32 devices in a mesh: groups: 2 (over y), wide: 4 (over z), narrow: 2 (over x), sub: 2 (over core).
Axes of the slice: x: 2, y: 2, z: 4, core: 2. Of those that a mesh axis runs over, the one named last changes fastest.
Arguments:
- tokens: bfloat16 [128, 16384], P(('groups', 'wide'), ('narrow', 'sub')), parts along dimension 0, may hold values from -6 to 6
- gate_weight: bfloat16 [16384, 6656], P(('narrow', 'sub'), 'wide'), may hold values from -0.046875 to 0.046875
- up_weight: bfloat16 [16384, 6656], P(('narrow', 'sub'), 'wide'), may hold values from -0.046875 to 0.046875
- hidden_grad: bfloat16 [128, 6656], P(('groups', 'narrow', 'sub'), 'wide'), parts along dimension 0, may hold values from -6 to 6
Outputs:
- hidden: bfloat16 [128, 6656], P(('groups', 'narrow', 'sub'), 'wide'), parts along dimension 0
- input_grad: bfloat16 [128, 16384], P(('groups', 'wide'), ('narrow', 'sub')), parts along dimension 0
The draws below stay inside these ranges and needn't reach their ends.
There are 2 independent parts, one for each index of `groups`. The reference program is written for one: setup_inputs(seed, part) draws one part's arguments, and reference() takes and returns one part's arrays. A program takes and returns all parts, laid end to end along the dimension named above; an argument that names none is the same for every part. Nothing has to cross between parts.
All inputs are finite; a program needn't handle non-finite values.
Results may differ from the reference program's by a relative error of at most 0.005.
Values may be sent and summed in bfloat16 or wider, within the bound.
No kernel may reach another device: no remote copies, remote signals or barrier semaphores. Data moves between devices by JAX's collectives and lax.ppermute only.
A program may use at most 128 MiB of HBM per device.

```python
import jax
import jax.numpy as jnp

D = 16384
FF = 6656
TOKENS = 64


def block_scale(stream_key, extent, pieces, low, top_value):
    level, own = 1.0, jax.random.fold_in(stream_key, 6)
    for dim, blocks in pieces:
        heights = jnp.exp(jax.random.uniform(jax.random.fold_in(own, dim), (blocks,), jnp.float32, low / len(pieces), top_value / len(pieces)))
        level = level * jnp.repeat(heights, extent[dim] // blocks).reshape([-1 if axis == dim else 1 for axis in range(len(extent))])
    return level


def noise(own_key, shape, deviation, limit, split=(), dtype=jnp.bfloat16):
    entries = jax.random.normal(own_key, shape, jnp.float32) * deviation
    if len(split) > 0:
        entries = block_scale(own_key, shape, split, -0.22, 0.18) * entries
    return jnp.clip(entries, min=-limit, max=limit).astype(dtype)


def setup_inputs(seed: int = 0, part: int = 0) -> dict:
    streams_of = jax.random.split(jax.random.key(seed), 5)
    own_keys = jax.random.split(jax.random.fold_in(streams_of[4], part), 5)
    return {
        "tokens": noise(own_keys[0], (TOKENS, D), 1.0, 6.0, ((0, 4), (1, 4))),
        "gate_weight": noise(streams_of[1], (D, FF), D ** -0.5, 0.046875, ((0, 4), (1, 4))),
        "up_weight": noise(streams_of[2], (D, FF), D ** -0.5, 0.046875, ((0, 4), (1, 4))),
        "hidden_grad": noise(own_keys[3], (TOKENS, FF), 1.0, 6.0, ((0, 4), (1, 4))),
    }


def reference(tokens, gate_weight, up_weight, hidden_grad):
    gate = jnp.dot(tokens, gate_weight, preferred_element_type=jnp.float32)
    up = jnp.dot(tokens, up_weight, preferred_element_type=jnp.float32)
    sig = 1.0 / (1.0 + jnp.exp(-gate))
    act = gate * sig
    hidden = (act * up).astype(jnp.bfloat16)
    grad = hidden_grad.astype(jnp.float32)
    pre_gate = (grad * up * sig * (1.0 + gate * (1.0 - sig))).astype(jnp.bfloat16)
    pre_up = (grad * act).astype(jnp.bfloat16)
    input_grad = jnp.dot(pre_gate, gate_weight.T, preferred_element_type=jnp.float32)
    input_grad = input_grad + jnp.dot(pre_up, up_weight.T, preferred_element_type=jnp.float32)
    input_grad = input_grad.astype(jnp.bfloat16)
    return (hidden, input_grad)
```

```python
import functools
import math

import jax
import jax.numpy as jnp
from jax import lax
from jax.experimental import pallas as pl
from jax.experimental.pallas import tpu as pltpu
from jax.sharding import PartitionSpec as P

VMEM = pl.BlockSpec(memory_space=pltpu.VMEM)
PARAMS = pltpu.CompilerParams(vmem_limit_bytes=8 << 20)
NT = (((1,), (1,)), ((), ()))


def partner(index, step, size):
    return index ^ step if size & (size - 1) == 0 else (index + step) % size


def source(index, step, size):
    return index ^ step if size & (size - 1) == 0 else (index + size - step) % size


def exchange(x, axis, step, size):
    return lax.ppermute(x, axis, [(i, partner(i, step, size)) for i in range(size)])


def tiles(width, tile=256):
    return width // tile, width // tile * tile


def load_weights(gate_weight, up_weight, parts=4):
    rows = gate_weight.shape[0]
    step = rows // parts

    def kernel(gate_hbm, up_hbm, gate_out, up_out, sems):
        copies = []
        for i in range(parts):
            span = pl.ds(i * step, step)
            copies.append(pltpu.make_async_copy(gate_hbm.at[span], gate_out.at[span], sems.at[2 * i]))
            copies.append(pltpu.make_async_copy(up_hbm.at[span], up_out.at[span], sems.at[2 * i + 1]))
        for copy in copies:
            copy.start()
        for copy in copies:
            copy.wait()

    shape = gate_weight.shape
    return pl.pallas_call(
        kernel,
        out_shape=[pltpu.VMEM(shape, jnp.bfloat16)] * 2,
        in_specs=[pl.BlockSpec(memory_space=pltpu.HBM)] * 2,
        out_specs=[VMEM] * 2,
        scratch_shapes=[pltpu.SemaphoreType.DMA((2 * parts,))],
        compiler_params=PARAMS,
        cost_estimate=pl.CostEstimate(flops=0, bytes_accessed=2 * 2 * gate_weight.size, transcendentals=0),
        name="load_weights",
    )(gate_weight, up_weight)


def forward(blocks, gate_weight, up_weight, sizes):
    wide, narrow, sub = sizes
    block_rows, depth = blocks[0].shape
    hidden_cols = gate_weight.shape[1]
    rows = block_rows * wide
    share = rows // (narrow * sub)
    piece = math.gcd(block_rows, share)
    half = rows // sub

    def kernel(*refs):
        block_refs = refs[:wide]
        gate_ref, up_ref, keep_ref, send_ref, x_ref = refs[wide:]
        me, core = lax.axis_index("wide"), lax.axis_index("sub")
        for step, block in enumerate(block_refs):
            owner = source(me, step, wide)
            for i in range(block_rows // piece):
                row = owner * block_rows + i * piece
                part = row // share
                place = ((part % sub) ^ core) * half + part // sub * share + row % share
                x_ref[pl.ds(pl.multiple_of(place, piece), piece), :] = block[pl.ds(i * piece, piece), :]

        def columns(weight, start, width, out):
            product = jnp.dot(x_ref[...], weight[:, pl.ds(start, width)], preferred_element_type=jnp.float32)
            keep_ref[:, pl.ds(out, width)] = product[:half]
            send_ref[:, pl.ds(out, width)] = product[half:]

        whole, rest = tiles(hidden_cols)
        for i, weight in enumerate((gate_ref, up_ref)):

            def body(t, carry, i=i, weight=weight):
                start = pl.multiple_of(t * 256, 256)
                columns(weight, start, 256, pl.multiple_of(start + i * hidden_cols, 128))
                return carry

            lax.fori_loop(0, whole, body, 0)
            if rest < hidden_cols:
                columns(weight, rest, hidden_cols - rest, rest + i * hidden_cols)

    shape = jax.ShapeDtypeStruct((half, 2 * hidden_cols), jnp.float32)
    return pl.pallas_call(
        kernel,
        out_shape=[shape] * 2,
        in_specs=[VMEM] * (wide + 2),
        out_specs=[VMEM] * 2,
        scratch_shapes=[pltpu.VMEM((rows, depth), jnp.bfloat16)],
        compiler_params=PARAMS,
        name="forward",
    )(*blocks, gate_weight, up_weight)


def activate(own, others, grads, sizes):
    wide, narrow, sub = sizes
    rows, both = own.shape
    hidden_cols = both // 2
    share = rows // narrow

    def kernel(*refs):
        own_ref = refs[0]
        other_refs = refs[1:narrow]
        grad_refs = refs[narrow : 2 * narrow]
        hidden_ref, pre_ref = refs[2 * narrow :]
        me = lax.axis_index("narrow")
        for step, grad_ref in enumerate(grad_refs):
            row = pl.ds(pl.multiple_of(source(me, step, narrow) * share, share), share)

            def total(cols, row=row):
                value = own_ref[row, cols]
                for other in other_refs:
                    value += other[row, cols].astype(jnp.float32)
                return value

            for start in range(0, hidden_cols, 128):
                cols = pl.ds(start, 128)
                up_cols = pl.ds(start + hidden_cols, 128)
                gate, up = total(cols), total(up_cols)
                sig = 1.0 / (1.0 + jnp.exp(-gate))
                act = gate * sig
                if step == 0:
                    hidden_ref[:, cols] = (act * up).astype(jnp.bfloat16)
                grad = grad_ref[:, cols].astype(jnp.float32)
                pre_ref[row, cols] = (grad * up * sig * (1.0 + gate * (1.0 - sig))).astype(jnp.bfloat16)
                pre_ref[row, up_cols] = (grad * act).astype(jnp.bfloat16)

    return pl.pallas_call(
        kernel,
        out_shape=[
            jax.ShapeDtypeStruct((share, hidden_cols), jnp.bfloat16),
            jax.ShapeDtypeStruct((rows, both), jnp.bfloat16),
        ],
        in_specs=[VMEM] * (2 * narrow),
        out_specs=[VMEM] * 2,
        compiler_params=PARAMS,
        name="activate",
    )(own, *others, *grads)


def backward(own, other, gate_weight, up_weight, sizes):
    wide, narrow, sub = sizes
    half, both = own.shape
    hidden_cols = both // 2
    rows = half * sub
    block_rows = rows // wide
    share = half // narrow
    piece = math.gcd(block_rows, share)
    depth = gate_weight.shape[0]

    def kernel(own_ref, other_ref, gate_ref, up_ref, *refs):
        out_refs, pre_ref = refs[:wide], refs[wide]
        me, core = lax.axis_index("wide"), lax.axis_index("sub")
        for flip, ref in enumerate((own_ref, other_ref)):
            for i in range(half // piece):
                row = (i * piece // share * sub + (core ^ flip)) * share + i * piece % share
                place = source(row // block_rows, me, wide) * block_rows + row % block_rows
                pre_ref[pl.ds(pl.multiple_of(place, piece), piece), :] = ref[pl.ds(i * piece, piece), :]

        def body(t, carry):
            cols = pl.ds(pl.multiple_of(t * 256, 256), 256)
            product = lax.dot_general(
                pre_ref[:, :hidden_cols], gate_ref[cols, :], NT, preferred_element_type=jnp.float32
            )
            product += lax.dot_general(
                pre_ref[:, hidden_cols:], up_ref[cols, :], NT, preferred_element_type=jnp.float32
            )
            for step, out in enumerate(out_refs):
                out[:, cols] = product[step * block_rows : (step + 1) * block_rows].astype(out.dtype)
            return carry

        lax.fori_loop(0, depth // 256, body, 0)

    return pl.pallas_call(
        kernel,
        out_shape=[
            jax.ShapeDtypeStruct((block_rows, depth), jnp.bfloat16 if step else jnp.float32)
            for step in range(wide)
        ],
        in_specs=[VMEM] * 4,
        out_specs=[VMEM] * wide,
        scratch_shapes=[pltpu.VMEM((rows, both), jnp.bfloat16)],
        compiler_params=PARAMS,
        name="backward",
    )(own, other, gate_weight, up_weight)


def shards(tokens, gate_weight, up_weight, hidden_grad, sizes):
    wide, narrow, sub = sizes
    order = [2, 3, 1] if wide == 4 else range(1, wide)
    got = {step: exchange(tokens, "wide", step, wide) for step in order}
    blocks = [tokens] + [got[step] for step in range(1, wide)]
    grads = [hidden_grad] + [exchange(hidden_grad, "narrow", step, narrow) for step in range(1, narrow)]
    gate_weight, up_weight = load_weights(gate_weight, up_weight)
    keep, send = forward(blocks, gate_weight, up_weight, sizes)
    chip = keep + exchange(send, "sub", 1, sub)
    chip_bf16 = chip.astype(jnp.bfloat16)
    others = [exchange(chip_bf16, "narrow", step, narrow) for step in range(1, narrow)]
    hidden, pre = activate(chip, others, grads, sizes)
    pre_other = exchange(pre, "sub", 1, sub)
    own, *sends = backward(pre, pre_other, gate_weight, up_weight, sizes)
    got = {step: exchange(sends[step - 1], "wide", step, wide) for step in order}
    input_grad = own
    for step in range(1, wide):
        input_grad = input_grad + got[step].astype(jnp.float32)
    return (hidden, input_grad.astype(jnp.bfloat16))


def solution(mesh):
    sizes = tuple(mesh.shape[axis] for axis in ("wide", "narrow", "sub"))
    return jax.shard_map(
        functools.partial(shards, sizes=sizes),
        mesh=mesh,
        in_specs=(
            P(("groups", "wide"), ("narrow", "sub")),
            P(("narrow", "sub"), "wide"),
            P(("narrow", "sub"), "wide"),
            P(("groups", "narrow", "sub"), "wide"),
        ),
        out_specs=(
            P(("groups", "narrow", "sub"), "wide"),
            P(("groups", "wide"), ("narrow", "sub")),
        ),
        check_vma=False,
    )
```

```python
import functools
import math

import jax
import jax.numpy as jnp
from jax import lax
from jax.experimental import pallas as pl
from jax.experimental.pallas import tpu as pltpu
from jax.sharding import PartitionSpec as P

VMEM = pl.BlockSpec(memory_space=pltpu.VMEM)
PARAMS = pltpu.CompilerParams(vmem_limit_bytes=8 << 20)
NT = (((1,), (1,)), ((), ()))


def partner(index, step, size):
    return index ^ step if size & (size - 1) == 0 else (index + step) % size


def source(index, step, size):
    return index ^ step if size & (size - 1) == 0 else (index + size - step) % size


def exchange(x, axis, step, size):
    return lax.ppermute(x, axis, [(i, partner(i, step, size)) for i in range(size)])


def tiles(width, tile=256):
    return width // tile, width // tile * tile


def load_turned(weight, next_weight, step=512):
    depth, hidden_cols = weight.shape
    step = math.gcd(depth, step)
    parts = depth // step
    ahead = ahead_rows(depth)

    def kernel(hbm_ref, next_hbm, out_ref, turned_ref, next_ref, sems):
        def copy(part):
            span = pl.ds(pl.multiple_of(part * step, step), step)
            return pltpu.make_async_copy(hbm_ref.at[span], out_ref.at[span], sems.at[part])

        for part in range(parts):
            copy(part).start()
        next_copy = pltpu.make_async_copy(next_hbm.at[pl.ds(0, ahead)], next_ref.at[pl.ds(0, ahead)], sems.at[parts])
        next_copy.start()

        def body(part, carry):
            span = pl.ds(pl.multiple_of(part * step, step), step)
            copy(part).wait()
            turned_ref[:, span] = out_ref[span, :].T
            return carry

        lax.fori_loop(0, parts, body, 0)
        next_copy.wait()

    shape = pltpu.VMEM((depth, hidden_cols), jnp.bfloat16)
    return pl.pallas_call(
        kernel,
        out_shape=[shape, pltpu.VMEM((hidden_cols, depth), jnp.bfloat16), shape],
        in_specs=[pl.BlockSpec(memory_space=pltpu.HBM)] * 2,
        out_specs=[VMEM] * 3,
        scratch_shapes=[pltpu.SemaphoreType.DMA((parts + 1,))],
        compiler_params=PARAMS,
        cost_estimate=pl.CostEstimate(flops=0, bytes_accessed=2 * weight.size, transcendentals=0),
        name="load_turned",
    )(weight, next_weight)


def ahead_rows(depth):
    return math.gcd(depth, 2048)


def turn(weight, step=512):
    depth, hidden_cols = weight.shape
    step = math.gcd(depth, step)

    def kernel(weight_ref, out_ref):
        def body(part, carry):
            span = pl.ds(pl.multiple_of(part * step, step), step)
            out_ref[:, span] = weight_ref[span, :].T
            return carry

        lax.fori_loop(0, depth // step, body, 0)

    return pl.pallas_call(
        kernel,
        out_shape=pltpu.VMEM((hidden_cols, depth), jnp.bfloat16),
        in_specs=[VMEM],
        out_specs=VMEM,
        compiler_params=PARAMS,
        cost_estimate=pl.CostEstimate(flops=0, bytes_accessed=2 * 2 * weight.size, transcendentals=0),
        name="turn",
    )(weight)


def forward(blocks, gate_weight, up_weight, up_buffer, held, sizes):
    wide, narrow, sub = sizes
    block_rows, depth = blocks[0].shape
    hidden_cols = gate_weight.shape[1]
    rows = block_rows * wide
    share = rows // (narrow * sub)
    piece = math.gcd(block_rows, share)
    half = rows // sub
    chunk = ahead_rows(depth)

    def kernel(*refs):
        block_refs = refs[:wide]
        gate_ref, up_hbm, _, _, keep_ref, send_ref, up_ref, x_ref, sems = refs[wide:]
        copies = []
        for i in range(1, depth // chunk):
            span = pl.ds(i * chunk, chunk)
            copies.append(pltpu.make_async_copy(up_hbm.at[span], up_ref.at[span], sems.at[i]))
            copies[-1].start()
        me, core = lax.axis_index("wide"), lax.axis_index("sub")
        for step, block in enumerate(block_refs):
            owner = source(me, step, wide)
            for i in range(block_rows // piece):
                row = owner * block_rows + i * piece
                part = row // share
                place = ((part % sub) ^ core) * half + part // sub * share + row % share
                x_ref[pl.ds(pl.multiple_of(place, piece), piece), :] = block[pl.ds(i * piece, piece), :]

        def columns(weight, start, out, first, last):
            for begin in range(0, hidden_cols, 256):
                width = min(256, hidden_cols - begin)
                product = jnp.dot(
                    x_ref[:, first:last], weight[first:last, begin : begin + width], preferred_element_type=jnp.float32
                )
                cols = pl.ds(out + begin, width)
                if first == start:
                    keep_ref[:, cols] = product[:half]
                    send_ref[:, cols] = product[half:]
                else:
                    keep_ref[:, cols] += product[:half]
                    send_ref[:, cols] += product[half:]

        columns(gate_ref, 0, 0, 0, depth)
        for i in range(depth // chunk):
            if i > 0:
                copies[i - 1].wait()
            columns(up_ref, 0, hidden_cols, i * chunk, (i + 1) * chunk)

    shape = jax.ShapeDtypeStruct((half, 2 * hidden_cols), jnp.float32)
    return pl.pallas_call(
        kernel,
        out_shape=[shape] * 2 + [pltpu.VMEM((depth, hidden_cols), jnp.bfloat16)],
        in_specs=[VMEM] * (wide + 1) + [pl.BlockSpec(memory_space=pltpu.HBM), VMEM, VMEM],
        input_output_aliases={wide + 2: 2},
        out_specs=[VMEM] * 3,
        scratch_shapes=[pltpu.VMEM((rows, depth), jnp.bfloat16), pltpu.SemaphoreType.DMA((depth // chunk,))],
        compiler_params=PARAMS,
        name="forward",
    )(*blocks, gate_weight, up_weight, up_buffer, held)


def activate(own, others, grads, sizes):
    wide, narrow, sub = sizes
    rows, both = own.shape
    hidden_cols = both // 2
    share = rows // narrow

    def kernel(*refs):
        own_ref = refs[0]
        other_refs = refs[1:narrow]
        grad_refs = refs[narrow : 2 * narrow]
        hidden_ref, pre_ref = refs[2 * narrow :]
        me = lax.axis_index("narrow")
        for step, grad_ref in enumerate(grad_refs):
            row = pl.ds(pl.multiple_of(source(me, step, narrow) * share, share), share)

            def total(cols, row=row):
                value = own_ref[row, cols]
                for other in other_refs:
                    value += other[row, cols].astype(jnp.float32)
                return value

            for start in range(0, hidden_cols, 128):
                cols = pl.ds(start, 128)
                up_cols = pl.ds(start + hidden_cols, 128)
                gate, up = total(cols), total(up_cols)
                sig = 1.0 / (1.0 + jnp.exp(-gate))
                act = gate * sig
                if step == 0:
                    hidden_ref[:, cols] = (act * up).astype(jnp.bfloat16)
                grad = grad_ref[:, cols].astype(jnp.float32)
                pre_ref[row, cols] = (grad * up * sig * (1.0 + gate * (1.0 - sig))).astype(jnp.bfloat16)
                pre_ref[row, up_cols] = (grad * act).astype(jnp.bfloat16)

    return pl.pallas_call(
        kernel,
        out_shape=[
            jax.ShapeDtypeStruct((share, hidden_cols), jnp.bfloat16),
            jax.ShapeDtypeStruct((rows, both), jnp.bfloat16),
        ],
        in_specs=[VMEM] * (2 * narrow),
        out_specs=[VMEM] * 2,
        compiler_params=PARAMS,
        name="activate",
    )(own, *others, *grads)


def backward(own, other, gate_turned, up_turned, begin, depth, groups, sizes):
    wide, narrow, sub = sizes
    half, both = own.shape
    hidden_cols = both // 2
    rows = half * sub
    block_rows = rows // wide
    share = half // narrow
    piece = math.gcd(block_rows, share)
    tile = math.gcd(depth, 512)

    def kernel(own_ref, other_ref, gate_ref, up_ref, *refs):
        out_refs, pre_ref = refs[:-1], refs[-1]
        me, core = lax.axis_index("wide"), lax.axis_index("sub")
        for flip, ref in enumerate((own_ref, other_ref)):
            for i in range(half // piece):
                row = (i * piece // share * sub + (core ^ flip)) * share + i * piece % share
                place = source(row // block_rows, me, wide) * block_rows + row % block_rows
                pre_ref[pl.ds(pl.multiple_of(place, piece), piece), :] = ref[pl.ds(i * piece, piece), :]

        for start in range(0, depth, tile):
            from_cols, cols = pl.ds(begin + start, tile), pl.ds(start, tile)
            product = jnp.dot(pre_ref[:, :hidden_cols], gate_ref[:, from_cols], preferred_element_type=jnp.float32)
            product += jnp.dot(pre_ref[:, hidden_cols:], up_ref[:, from_cols], preferred_element_type=jnp.float32)
            for (steps, dtype), out in zip(groups, out_refs):
                for i, step in enumerate(steps):
                    block = product[step * block_rows : (step + 1) * block_rows].astype(dtype)
                    out[i * block_rows : (i + 1) * block_rows, cols] = block

    return pl.pallas_call(
        kernel,
        out_shape=[jax.ShapeDtypeStruct((len(steps) * block_rows, depth), dtype) for steps, dtype in groups],
        in_specs=[VMEM] * 4,
        out_specs=[VMEM] * len(groups),
        scratch_shapes=[pltpu.VMEM((rows, both), jnp.bfloat16)],
        compiler_params=PARAMS,
        cost_estimate=pl.CostEstimate(
            flops=2 * rows * both * depth, bytes_accessed=2 * both * depth, transcendentals=0
        ),
        name="backward",
    )(own, other, gate_turned, up_turned)


def shards(tokens, gate_weight, up_weight, hidden_grad, sizes):
    wide, narrow, sub = sizes
    order = list(AG_ORDER) if wide == 4 else list(range(1, wide))
    got = {step: exchange(tokens, "wide", step, wide) for step in order}
    blocks = [tokens] + [got[step] for step in range(1, wide)]
    gate_weight = pltpu.with_memory_space_constraint(gate_weight, pltpu.HBM)
    up_weight = pltpu.with_memory_space_constraint(up_weight, pltpu.HBM)
    grads = [hidden_grad] + [exchange(hidden_grad, "narrow", step, narrow) for step in range(1, narrow)]
    gate_weight, gate_turned, up_buffer = load_turned(gate_weight, up_weight)
    blocks, grads = lax.optimization_barrier((blocks, grads))
    keep, send, up_weight = forward(blocks, gate_weight, up_weight, up_buffer, gate_turned, sizes)
    chip = keep + exchange(send, "sub", 1, sub)
    chip_bf16 = chip.astype(jnp.bfloat16)
    up_weight, chip_bf16 = lax.optimization_barrier((up_weight, chip_bf16))
    others = [exchange(chip_bf16, "narrow", step, narrow) for step in range(1, narrow)]
    up_turned = turn(up_weight)
    others, up_turned = lax.optimization_barrier((others, up_turned))
    hidden, pre = activate(chip, others, grads, sizes)
    pre_other = exchange(pre, "sub", 1, sub)

    order = list(RS_ORDER) if wide == 4 else list(range(1, wide))
    f32, bf16 = jnp.float32, jnp.bfloat16
    bwd = functools.partial(backward, pre, pre_other, gate_turned, up_turned, sizes=sizes)
    direct = [((0,), f32)] + [((step,), bf16) for step in order]
    depth = tokens.shape[1]
    widths = [depth * share // sum(SHARES) for share in SHARES]
    begins = [sum(widths[:i]) for i in range(len(widths))]
    totals, owns, sends = [], [], []
    for begin, width in zip(begins, widths):
        own, *send = bwd(begin=begin, depth=width, groups=direct)
        owns.append(own)
        sends.append(dict(zip(order, send)))
    whole = {}
    if MERGE:
        whole[1] = exchange(jnp.concatenate([send.pop(1) for send in sends], axis=1), "wide", 1, wide)
    got = [{step: exchange(x, "wide", step, wide) for step, x in send.items()} for send in sends]
    for begin, width, own, parts in zip(begins, widths, owns, got):
        parts.update({step: x[:, begin : begin + width] for step, x in whole.items()})
        totals.append(own + sum(x.astype(f32) for x in parts.values()))
    return (hidden, jnp.concatenate([total.astype(bf16) for total in totals], axis=1))


SHARES = (1, 1)
AG_ORDER = (2, 3, 1)
RS_ORDER = (3, 1, 2)
RELAY = False
MERGE = False


def solution(mesh):
    sizes = tuple(mesh.shape[axis] for axis in ("wide", "narrow", "sub"))
    return jax.shard_map(
        functools.partial(shards, sizes=sizes),
        mesh=mesh,
        in_specs=(
            P(("groups", "wide"), ("narrow", "sub")),
            P(("narrow", "sub"), "wide"),
            P(("narrow", "sub"), "wide"),
            P(("groups", "narrow", "sub"), "wide"),
        ),
        out_specs=(
            P(("groups", "narrow", "sub"), "wide"),
            P(("groups", "wide"), ("narrow", "sub")),
        ),
        check_vma=False,
    )
```

```python
import functools
import math

import jax
import jax.numpy as jnp
from jax import lax
from jax.experimental import pallas as pl
from jax.experimental.pallas import tpu as pltpu
from jax.sharding import PartitionSpec as P

VMEM = pl.BlockSpec(memory_space=pltpu.VMEM)
PARAMS = pltpu.CompilerParams(vmem_limit_bytes=8 << 20)
NT = (((1,), (1,)), ((), ()))


def partner(index, step, size):
    return index ^ step if size & (size - 1) == 0 else (index + step) % size


def source(index, step, size):
    return index ^ step if size & (size - 1) == 0 else (index + size - step) % size


def exchange(x, axis, step, size):
    return lax.ppermute(x, axis, [(i, partner(i, step, size)) for i in range(size)])


def tiles(width, tile=256):
    return width // tile, width // tile * tile


def load_turned(weight, next_weight, step=512):
    depth, hidden_cols = weight.shape
    step = math.gcd(depth, step)
    parts = depth // step
    ahead = ahead_rows(depth)

    def kernel(hbm_ref, next_hbm, out_ref, turned_ref, next_ref, sems):
        def copy(part):
            span = pl.ds(pl.multiple_of(part * step, step), step)
            return pltpu.make_async_copy(hbm_ref.at[span], out_ref.at[span], sems.at[part])

        for part in range(parts):
            copy(part).start()
        next_copy = pltpu.make_async_copy(next_hbm.at[pl.ds(0, ahead)], next_ref.at[pl.ds(0, ahead)], sems.at[parts])
        next_copy.start()

        def body(part, carry):
            span = pl.ds(pl.multiple_of(part * step, step), step)
            copy(part).wait()
            turned_ref[:, span] = out_ref[span, :].T
            return carry

        lax.fori_loop(0, parts, body, 0)
        next_copy.wait()

    shape = pltpu.VMEM((depth, hidden_cols), jnp.bfloat16)
    return pl.pallas_call(
        kernel,
        out_shape=[shape, pltpu.VMEM((hidden_cols, depth), jnp.bfloat16), shape],
        in_specs=[pl.BlockSpec(memory_space=pltpu.HBM)] * 2,
        out_specs=[VMEM] * 3,
        scratch_shapes=[pltpu.SemaphoreType.DMA((parts + 1,))],
        compiler_params=PARAMS,
        cost_estimate=pl.CostEstimate(flops=0, bytes_accessed=2 * weight.size, transcendentals=0),
        name="load_turned",
    )(weight, next_weight)


def ahead_rows(depth):
    return depth * AHEAD // 4


def turn(weight, step=512):
    depth, hidden_cols = weight.shape
    step = math.gcd(depth, step)

    def kernel(weight_ref, out_ref):
        def body(part, carry):
            span = pl.ds(pl.multiple_of(part * step, step), step)
            out_ref[:, span] = weight_ref[span, :].T
            return carry

        lax.fori_loop(0, depth // step, body, 0)

    return pl.pallas_call(
        kernel,
        out_shape=pltpu.VMEM((hidden_cols, depth), jnp.bfloat16),
        in_specs=[VMEM],
        out_specs=VMEM,
        compiler_params=PARAMS,
        cost_estimate=pl.CostEstimate(flops=0, bytes_accessed=2 * 2 * weight.size, transcendentals=0),
        name="turn",
    )(weight)


def forward(steps, blocks, gate_weight, up_weight, up_buffer, held, sizes):
    wide, narrow, sub = sizes
    block_rows, depth = blocks[0].shape
    hidden_cols = gate_weight.shape[1]
    rows = block_rows * wide
    share = rows // (narrow * sub)
    piece = math.gcd(block_rows, share)
    half = rows // sub
    ahead = ahead_rows(depth)

    def kernel(*refs):
        block_refs = refs[:wide]
        gate_ref, up_hbm, _, _, keep_ref, send_ref, up_ref, x_ref, sem = refs[wide:]
        span = pl.ds(ahead, depth - ahead)
        rest = pltpu.make_async_copy(up_hbm.at[span], up_ref.at[span], sem)
        rest.start()
        me, core = lax.axis_index("wide"), lax.axis_index("sub")
        for step, block in zip(steps, block_refs):
            owner = source(me, step, wide)
            for i in range(block_rows // piece):
                row = owner * block_rows + i * piece
                part = row // share
                place = ((part % sub) ^ core) * half + part // sub * share + row % share
                x_ref[pl.ds(pl.multiple_of(place, piece), piece), :] = block[pl.ds(i * piece, piece), :]

        def columns(weight, out):
            for begin in range(0, hidden_cols, 256):
                width = min(256, hidden_cols - begin)
                product = jnp.dot(x_ref[...], weight[:, begin : begin + width], preferred_element_type=jnp.float32)
                cols = pl.ds(out + begin, width)
                keep_ref[:, cols] = product[:half]
                send_ref[:, cols] = product[half:].astype(send_ref.dtype)

        columns(gate_ref, 0)
        rest.wait()
        columns(up_ref, hidden_cols)

    shape = (half, 2 * hidden_cols)
    return pl.pallas_call(
        kernel,
        out_shape=[
            jax.ShapeDtypeStruct(shape, jnp.float32),
            jax.ShapeDtypeStruct(shape, SUB_DTYPE),
            pltpu.VMEM((depth, hidden_cols), jnp.bfloat16),
        ],
        in_specs=[VMEM] * (wide + 1) + [pl.BlockSpec(memory_space=pltpu.HBM), VMEM, VMEM],
        input_output_aliases={wide + 2: 2},
        out_specs=[VMEM] * 3,
        scratch_shapes=[pltpu.VMEM((rows, depth), jnp.bfloat16), pltpu.SemaphoreType.DMA(())],
        compiler_params=PARAMS,
        name="forward",
    )(*blocks, gate_weight, up_weight, up_buffer, held)


def activate(own, others, grads, sizes):
    wide, narrow, sub = sizes
    rows, both = own.shape
    hidden_cols = both // 2
    share = rows // narrow

    def kernel(*refs):
        own_ref = refs[0]
        other_refs = refs[1:narrow]
        grad_refs = refs[narrow : 2 * narrow]
        hidden_ref, pre_ref = refs[2 * narrow :]
        me = lax.axis_index("narrow")
        for step, grad_ref in enumerate(grad_refs):
            row = pl.ds(pl.multiple_of(source(me, step, narrow) * share, share), share)

            def total(cols, row=row):
                value = own_ref[row, cols]
                for other in other_refs:
                    value += other[row, cols].astype(jnp.float32)
                return value

            for start in range(0, hidden_cols, 128):
                cols = pl.ds(start, 128)
                up_cols = pl.ds(start + hidden_cols, 128)
                gate, up = total(cols), total(up_cols)
                sig = 1.0 / (1.0 + jnp.exp(-gate))
                act = gate * sig
                if step == 0:
                    hidden_ref[:, cols] = (act * up).astype(jnp.bfloat16)
                grad = grad_ref[:, cols].astype(jnp.float32)
                pre_ref[row, cols] = (grad * up * sig * (1.0 + gate * (1.0 - sig))).astype(jnp.bfloat16)
                pre_ref[row, up_cols] = (grad * act).astype(jnp.bfloat16)

    return pl.pallas_call(
        kernel,
        out_shape=[
            pltpu.VMEM((share, hidden_cols), jnp.bfloat16),
            jax.ShapeDtypeStruct((rows, both), jnp.bfloat16),
        ],
        in_specs=[VMEM] * (2 * narrow),
        out_specs=[VMEM] * 2,
        compiler_params=PARAMS,
        name="activate",
    )(own, *others, *grads)


def backward(own, other, gate_turned, up_turned, begin, depth, groups, sizes):
    wide, narrow, sub = sizes
    half, both = own.shape
    hidden_cols = both // 2
    rows = half * sub
    block_rows = rows // wide
    share = half // narrow
    piece = math.gcd(block_rows, share)
    tile = math.gcd(depth, 512)

    def kernel(own_ref, other_ref, gate_ref, up_ref, *refs):
        out_refs, pre_ref = refs[:-1], refs[-1]
        me, core = lax.axis_index("wide"), lax.axis_index("sub")
        for flip, ref in enumerate((own_ref, other_ref)):
            for i in range(half // piece):
                row = (i * piece // share * sub + (core ^ flip)) * share + i * piece % share
                place = source(row // block_rows, me, wide) * block_rows + row % block_rows
                pre_ref[pl.ds(pl.multiple_of(place, piece), piece), :] = ref[pl.ds(i * piece, piece), :]

        for start in range(0, depth, tile):
            from_cols, cols = pl.ds(begin + start, tile), pl.ds(start, tile)
            product = jnp.dot(pre_ref[:, :hidden_cols], gate_ref[:, from_cols], preferred_element_type=jnp.float32)
            product += jnp.dot(pre_ref[:, hidden_cols:], up_ref[:, from_cols], preferred_element_type=jnp.float32)
            for (steps, dtype), out in zip(groups, out_refs):
                for i, step in enumerate(steps):
                    block = product[step * block_rows : (step + 1) * block_rows].astype(dtype)
                    out[i * block_rows : (i + 1) * block_rows, cols] = block

    return pl.pallas_call(
        kernel,
        out_shape=[jax.ShapeDtypeStruct((len(steps) * block_rows, depth), dtype) for steps, dtype in groups],
        in_specs=[VMEM] * 4,
        out_specs=[VMEM] * len(groups),
        scratch_shapes=[pltpu.VMEM((rows, both), jnp.bfloat16)],
        compiler_params=PARAMS,
        cost_estimate=pl.CostEstimate(
            flops=2 * rows * both * depth, bytes_accessed=2 * both * depth, transcendentals=0
        ),
        name="backward",
    )(own, other, gate_turned, up_turned)


def shards(tokens, gate_weight, up_weight, hidden_grad, sizes):
    wide, narrow, sub = sizes
    order = list(AG_ORDER) if wide == 4 else list(range(1, wide))
    got = {step: exchange(tokens, "wide", step, wide) for step in order}
    steps = [0] + order
    blocks = [tokens] + [got[step] for step in order]
    gate_weight = pltpu.with_memory_space_constraint(gate_weight, pltpu.HBM)
    up_weight = pltpu.with_memory_space_constraint(up_weight, pltpu.HBM)
    grads = [hidden_grad] + [exchange(hidden_grad, "narrow", step, narrow) for step in range(1, narrow)]
    gate_weight, gate_turned, up_buffer = load_turned(gate_weight, up_weight)
    blocks, grads = lax.optimization_barrier((blocks, grads))
    keep, send, up_weight = forward(steps, blocks, gate_weight, up_weight, up_buffer, gate_turned, sizes)
    chip = keep + exchange(send, "sub", 1, sub).astype(jnp.float32)
    chip_bf16 = chip.astype(jnp.bfloat16)
    up_weight, chip_bf16 = lax.optimization_barrier((up_weight, chip_bf16))
    others = [exchange(chip_bf16, "narrow", step, narrow) for step in range(1, narrow)]
    up_turned = turn(up_weight)
    others, up_turned = lax.optimization_barrier((others, up_turned))
    hidden, pre = activate(chip, others, grads, sizes)
    pre_other = exchange(pre, "sub", 1, sub)

    order = list(RS_ORDER) if wide == 4 else list(range(1, wide))
    f32, bf16 = jnp.float32, jnp.bfloat16
    bwd = functools.partial(backward, pre, pre_other, gate_turned, up_turned, sizes=sizes)
    direct = [((0,), f32)] + [((step,), bf16) for step in order]
    depth = tokens.shape[1]
    widths = [depth * share // sum(SHARES) for share in SHARES]
    begins = [sum(widths[:i]) for i in range(len(widths))]
    totals, owns, sends = [], [], []
    for begin, width in zip(begins, widths):
        own, *send = bwd(begin=begin, depth=width, groups=direct)
        owns.append(own)
        sends.append(dict(zip(order, send)))
    whole = {}
    if MERGE:
        whole[1] = exchange(jnp.concatenate([send.pop(1) for send in sends], axis=1), "wide", 1, wide)
    got = [{step: exchange(x, "wide", step, wide) for step, x in send.items()} for send in sends]
    for begin, width, own, parts in zip(begins, widths, owns, got):
        parts.update({step: x[:, begin : begin + width] for step, x in whole.items()})
        totals.append(own + sum(x.astype(f32) for x in parts.values()))
    return (hidden, jnp.concatenate([total.astype(bf16) for total in totals], axis=1))


SUB_DTYPE = jnp.bfloat16
AHEAD = 3
SHARES = (1, 1)
AG_ORDER = (3, 2, 1)
RS_ORDER = (3, 1, 2)
RELAY = False
MERGE = False


def solution(mesh):
    sizes = tuple(mesh.shape[axis] for axis in ("wide", "narrow", "sub"))
    return jax.shard_map(
        functools.partial(shards, sizes=sizes),
        mesh=mesh,
        in_specs=(
            P(("groups", "wide"), ("narrow", "sub")),
            P(("narrow", "sub"), "wide"),
            P(("narrow", "sub"), "wide"),
            P(("groups", "narrow", "sub"), "wide"),
        ),
        out_specs=(
            P(("groups", "narrow", "sub"), "wide"),
            P(("groups", "wide"), ("narrow", "sub")),
        ),
        check_vma=False,
    )
```

```python
import functools
import math

import jax
import jax.numpy as jnp
from jax import lax
from jax.experimental import pallas as pl
from jax.experimental.pallas import tpu as pltpu
from jax.sharding import PartitionSpec as P

VMEM = pl.BlockSpec(memory_space=pltpu.VMEM)
PARAMS = pltpu.CompilerParams(vmem_limit_bytes=8 << 20)
PARTS = 2


def partner(index, step, size):
    return index ^ step if size & (size - 1) == 0 else (index + step) % size


def source(index, step, size):
    return index ^ step if size & (size - 1) == 0 else (index + size - step) % size


def exchange(x, axis, step, size):
    return lax.ppermute(x, axis, [(i, partner(i, step, size)) for i in range(size)])


def load_turned(weight, next_weight, step=512):
    depth, hidden_cols = weight.shape
    step = math.gcd(depth, step)
    parts = depth // step
    ahead = ahead_rows(depth)

    def kernel(hbm_ref, next_hbm, out_ref, turned_ref, next_ref, sems):
        def copy(part):
            span = pl.ds(pl.multiple_of(part * step, step), step)
            return pltpu.make_async_copy(hbm_ref.at[span], out_ref.at[span], sems.at[part])

        for part in range(parts):
            copy(part).start()
        next_copy = pltpu.make_async_copy(next_hbm.at[pl.ds(0, ahead)], next_ref.at[pl.ds(0, ahead)], sems.at[parts])
        next_copy.start()

        def body(part, carry):
            span = pl.ds(pl.multiple_of(part * step, step), step)
            copy(part).wait()
            turned_ref[:, span] = out_ref[span, :].T
            return carry

        lax.fori_loop(0, parts, body, 0)
        next_copy.wait()

    shape = pltpu.VMEM((depth, hidden_cols), jnp.bfloat16)
    return pl.pallas_call(
        kernel,
        out_shape=[shape, pltpu.VMEM((hidden_cols, depth), jnp.bfloat16), shape],
        in_specs=[pl.BlockSpec(memory_space=pltpu.HBM)] * 2,
        out_specs=[VMEM] * 3,
        scratch_shapes=[pltpu.SemaphoreType.DMA((parts + 1,))],
        compiler_params=PARAMS,
        cost_estimate=pl.CostEstimate(flops=0, bytes_accessed=2 * weight.size, transcendentals=0),
        name="load_turned",
    )(weight, next_weight)


def ahead_rows(depth):
    return depth * 3 // 4


def turn(weight, step=512):
    depth, hidden_cols = weight.shape
    step = math.gcd(depth, step)

    def kernel(weight_ref, out_ref):
        def body(part, carry):
            span = pl.ds(pl.multiple_of(part * step, step), step)
            out_ref[:, span] = weight_ref[span, :].T
            return carry

        lax.fori_loop(0, depth // step, body, 0)

    return pl.pallas_call(
        kernel,
        out_shape=pltpu.VMEM((hidden_cols, depth), jnp.bfloat16),
        in_specs=[VMEM],
        out_specs=VMEM,
        compiler_params=PARAMS,
        cost_estimate=pl.CostEstimate(flops=0, bytes_accessed=2 * 2 * weight.size, transcendentals=0),
        name="turn",
    )(weight)


def forward(steps, blocks, gate_weight, up_weight, up_buffer, held, sizes):
    wide, narrow, sub = sizes
    block_rows, depth = blocks[0].shape
    hidden_cols = gate_weight.shape[1]
    rows = block_rows * wide
    share = rows // (narrow * sub)
    piece = math.gcd(block_rows, share)
    half = rows // sub
    ahead = ahead_rows(depth)

    def kernel(*refs):
        block_refs = refs[:wide]
        gate_ref, up_hbm, _, _, keep_ref, send_ref, up_ref, x_ref, sem = refs[wide:]
        span = pl.ds(ahead, depth - ahead)
        rest = pltpu.make_async_copy(up_hbm.at[span], up_ref.at[span], sem)
        rest.start()
        me, core = lax.axis_index("wide"), lax.axis_index("sub")
        for step, block in zip(steps, block_refs):
            owner = source(me, step, wide)
            for i in range(block_rows // piece):
                row = owner * block_rows + i * piece
                part = row // share
                place = ((part % sub) ^ core) * half + part // sub * share + row % share
                x_ref[pl.ds(pl.multiple_of(place, piece), piece), :] = block[pl.ds(i * piece, piece), :]

        def columns(weight, out):
            for begin in range(0, hidden_cols, 512):
                width = min(512, hidden_cols - begin)
                product = jnp.dot(x_ref[...], weight[:, begin : begin + width], preferred_element_type=jnp.float32)
                cols = pl.ds(out + begin, width)
                keep_ref[:, cols] = product[:half]
                send_ref[:, cols] = product[half:].astype(send_ref.dtype)

        columns(gate_ref, 0)
        rest.wait()
        columns(up_ref, hidden_cols)

    shape = (half, 2 * hidden_cols)
    return pl.pallas_call(
        kernel,
        out_shape=[
            jax.ShapeDtypeStruct(shape, jnp.float32),
            jax.ShapeDtypeStruct(shape, jnp.bfloat16),
            pltpu.VMEM((depth, hidden_cols), jnp.bfloat16),
        ],
        in_specs=[VMEM] * (wide + 1) + [pl.BlockSpec(memory_space=pltpu.HBM), VMEM, VMEM],
        input_output_aliases={wide + 2: 2},
        out_specs=[VMEM] * 3,
        scratch_shapes=[pltpu.VMEM((rows, depth), jnp.bfloat16), pltpu.SemaphoreType.DMA(())],
        compiler_params=PARAMS,
        name="forward",
    )(*blocks, gate_weight, up_weight, up_buffer, held)


def activate(own, others, grads, sizes):
    wide, narrow, sub = sizes
    rows, both = own.shape
    hidden_cols = both // 2
    share = rows // narrow

    def kernel(*refs):
        own_ref = refs[0]
        other_refs = refs[1:narrow]
        grad_refs = refs[narrow : 2 * narrow]
        hidden_ref, pre_ref = refs[2 * narrow :]
        me = lax.axis_index("narrow")
        for step, grad_ref in enumerate(grad_refs):
            row = pl.ds(pl.multiple_of(source(me, step, narrow) * share, share), share)

            def total(cols, row=row):
                value = own_ref[row, cols]
                for other in other_refs:
                    value += other[row, cols].astype(jnp.float32)
                return value

            for start in range(0, hidden_cols, 128):
                cols = pl.ds(start, 128)
                up_cols = pl.ds(start + hidden_cols, 128)
                gate, up = total(cols), total(up_cols)
                sig = 1.0 / (1.0 + jnp.exp(-gate))
                act = gate * sig
                if step == 0:
                    hidden_ref[:, cols] = (act * up).astype(jnp.bfloat16)
                grad = grad_ref[:, cols].astype(jnp.float32)
                pre_ref[row, cols] = (grad * up * sig * (1.0 + gate * (1.0 - sig))).astype(jnp.bfloat16)
                pre_ref[row, up_cols] = (grad * act).astype(jnp.bfloat16)

    return pl.pallas_call(
        kernel,
        out_shape=[
            pltpu.VMEM((share, hidden_cols), jnp.bfloat16),
            jax.ShapeDtypeStruct((rows, both), jnp.bfloat16),
        ],
        in_specs=[VMEM] * (2 * narrow),
        out_specs=[VMEM] * 2,
        compiler_params=PARAMS,
        name="activate",
    )(own, *others, *grads)


def backward(own, other, gate_turned, up_turned, begin, depth, groups, sizes):
    wide, narrow, sub = sizes
    half, both = own.shape
    hidden_cols = both // 2
    rows = half * sub
    block_rows = rows // wide
    share = half // narrow
    piece = math.gcd(block_rows, share)
    tile = math.gcd(depth, 512)

    def kernel(own_ref, other_ref, gate_ref, up_ref, *refs):
        out_refs, pre_ref = refs[:-1], refs[-1]
        me, core = lax.axis_index("wide"), lax.axis_index("sub")
        for flip, ref in enumerate((own_ref, other_ref)):
            for i in range(half // piece):
                row = (i * piece // share * sub + (core ^ flip)) * share + i * piece % share
                place = source(row // block_rows, me, wide) * block_rows + row % block_rows
                pre_ref[pl.ds(pl.multiple_of(place, piece), piece), :] = ref[pl.ds(i * piece, piece), :]

        for start in range(0, depth, tile):
            from_cols, cols = pl.ds(begin + start, tile), pl.ds(start, tile)
            product = jnp.dot(pre_ref[:, :hidden_cols], gate_ref[:, from_cols], preferred_element_type=jnp.float32)
            product += jnp.dot(pre_ref[:, hidden_cols:], up_ref[:, from_cols], preferred_element_type=jnp.float32)
            for (steps, dtype), out in zip(groups, out_refs):
                for i, step in enumerate(steps):
                    block = product[step * block_rows : (step + 1) * block_rows].astype(dtype)
                    out[i * block_rows : (i + 1) * block_rows, cols] = block

    return pl.pallas_call(
        kernel,
        out_shape=[jax.ShapeDtypeStruct((len(steps) * block_rows, depth), dtype) for steps, dtype in groups],
        in_specs=[VMEM] * 4,
        out_specs=[VMEM] * len(groups),
        scratch_shapes=[pltpu.VMEM((rows, both), jnp.bfloat16)],
        compiler_params=PARAMS,
        cost_estimate=pl.CostEstimate(
            flops=2 * rows * both * depth, bytes_accessed=2 * both * depth, transcendentals=0
        ),
        name="backward",
    )(own, other, gate_turned, up_turned)


def shards(tokens, gate_weight, up_weight, hidden_grad, sizes):
    wide, narrow, sub = sizes
    order = [3, 2, 1] if wide == 4 else list(range(1, wide))
    got = {step: exchange(tokens, "wide", step, wide) for step in order}
    steps = [0] + order
    blocks = [tokens] + [got[step] for step in order]
    gate_weight = pltpu.with_memory_space_constraint(gate_weight, pltpu.HBM)
    up_weight = pltpu.with_memory_space_constraint(up_weight, pltpu.HBM)
    grads = [hidden_grad] + [exchange(hidden_grad, "narrow", step, narrow) for step in range(1, narrow)]
    gate_weight, gate_turned, up_buffer = load_turned(gate_weight, up_weight)
    blocks, grads = lax.optimization_barrier((blocks, grads))
    keep, send, up_weight = forward(steps, blocks, gate_weight, up_weight, up_buffer, gate_turned, sizes)
    chip = keep + exchange(send, "sub", 1, sub).astype(jnp.float32)
    chip_bf16 = chip.astype(jnp.bfloat16)
    up_weight, chip_bf16 = lax.optimization_barrier((up_weight, chip_bf16))
    others = [exchange(chip_bf16, "narrow", step, narrow) for step in range(1, narrow)]
    up_turned = turn(up_weight)
    others, up_turned = lax.optimization_barrier((others, up_turned))
    hidden, pre = activate(chip, others, grads, sizes)
    pre_other = exchange(pre, "sub", 1, sub)

    order = list(range(1, wide))
    f32, bf16 = jnp.float32, jnp.bfloat16
    bwd = functools.partial(backward, pre, pre_other, gate_turned, up_turned, sizes=sizes)
    direct = [((0,), f32)] + [((step,), bf16) for step in order]
    width = tokens.shape[1] // PARTS
    totals = []
    for part in range(PARTS):
        own, *sends = bwd(begin=part * width, depth=width, groups=direct)
        sends = dict(zip(order, sends))
        turns = [3, 1, 2] if wide == 4 else order
        got = [exchange(sends[step], "wide", step, wide) for step in turns]
        totals.append(own + sum(x.astype(f32) for x in got))
    return (hidden, jnp.concatenate([total.astype(bf16) for total in totals], axis=1))


def solution(mesh):
    sizes = tuple(mesh.shape[axis] for axis in ("wide", "narrow", "sub"))
    return jax.shard_map(
        functools.partial(shards, sizes=sizes),
        mesh=mesh,
        in_specs=(
            P(("groups", "wide"), ("narrow", "sub")),
            P(("narrow", "sub"), "wide"),
            P(("narrow", "sub"), "wide"),
            P(("groups", "narrow", "sub"), "wide"),
        ),
        out_specs=(
            P(("groups", "narrow", "sub"), "wide"),
            P(("groups", "wide"), ("narrow", "sub")),
        ),
        check_vma=False,
    )
```

```python
import functools
import math

import jax
import jax.numpy as jnp
from jax import lax
from jax.experimental import pallas as pl
from jax.experimental.pallas import tpu as pltpu
from jax.sharding import PartitionSpec as P

VMEM = pl.BlockSpec(memory_space=pltpu.VMEM)
PARAMS = pltpu.CompilerParams(vmem_limit_bytes=8 << 20)
PARTS = 2


def partner(index, step, size):
    return index ^ step if size & (size - 1) == 0 else (index + step) % size


def source(index, step, size):
    return index ^ step if size & (size - 1) == 0 else (index + size - step) % size


def exchange(x, axis, step, size):
    return lax.ppermute(x, axis, [(i, partner(i, step, size)) for i in range(size)])


def load_turned(weight, next_weight, step=512):
    depth, hidden_cols = weight.shape
    step = math.gcd(depth, step)
    parts = depth // step
    ahead = ahead_rows(depth)

    def kernel(hbm_ref, next_hbm, out_ref, turned_ref, next_ref, sems):
        def copy(part):
            span = pl.ds(pl.multiple_of(part * step, step), step)
            return pltpu.make_async_copy(hbm_ref.at[span], out_ref.at[span], sems.at[part])

        for part in range(parts):
            copy(part).start()
        next_copy = pltpu.make_async_copy(next_hbm.at[pl.ds(0, ahead)], next_ref.at[pl.ds(0, ahead)], sems.at[parts])
        next_copy.start()

        def body(part, carry):
            span = pl.ds(pl.multiple_of(part * step, step), step)
            copy(part).wait()
            turned_ref[:, span] = out_ref[span, :].T
            return carry

        lax.fori_loop(0, parts, body, 0)
        next_copy.wait()

    shape = pltpu.VMEM((depth, hidden_cols), jnp.bfloat16)
    return pl.pallas_call(
        kernel,
        out_shape=[shape, pltpu.VMEM((hidden_cols, depth), jnp.bfloat16), shape],
        in_specs=[pl.BlockSpec(memory_space=pltpu.HBM)] * 2,
        out_specs=[VMEM] * 3,
        scratch_shapes=[pltpu.SemaphoreType.DMA((parts + 1,))],
        compiler_params=PARAMS,
        cost_estimate=pl.CostEstimate(flops=0, bytes_accessed=2 * weight.size, transcendentals=0),
        name="load_turned",
    )(weight, next_weight)


def ahead_rows(depth):
    return depth * 3 // 4


def turn(weight, step=2048):
    depth, hidden_cols = weight.shape
    step = math.gcd(depth, step)

    def kernel(weight_ref, out_ref):
        def body(part, carry):
            span = pl.ds(pl.multiple_of(part * step, step), step)
            out_ref[:, span] = weight_ref[span, :].T
            return carry

        lax.fori_loop(0, depth // step, body, 0)

    return pl.pallas_call(
        kernel,
        out_shape=pltpu.VMEM((hidden_cols, depth), jnp.bfloat16),
        in_specs=[VMEM],
        out_specs=VMEM,
        compiler_params=PARAMS,
        cost_estimate=pl.CostEstimate(flops=0, bytes_accessed=2 * 2 * weight.size, transcendentals=0),
        name="turn",
    )(weight)


def forward(steps, blocks, gate_weight, up_weight, up_buffer, held, sizes):
    wide, narrow, sub = sizes
    block_rows, depth = blocks[0].shape
    hidden_cols = gate_weight.shape[1]
    rows = block_rows * wide
    share = rows // (narrow * sub)
    piece = math.gcd(block_rows, share)
    half = rows // sub
    ahead = ahead_rows(depth)

    def kernel(*refs):
        block_refs = refs[:wide]
        gate_ref, up_hbm, _, _, keep_ref, send_ref, up_ref, x_ref, sem = refs[wide:]
        span = pl.ds(ahead, depth - ahead)
        rest = pltpu.make_async_copy(up_hbm.at[span], up_ref.at[span], sem)
        rest.start()
        me, core = lax.axis_index("wide"), lax.axis_index("sub")
        for step, block in zip(steps, block_refs):
            owner = source(me, step, wide)
            for i in range(block_rows // piece):
                row = owner * block_rows + i * piece
                part = row // share
                place = ((part % sub) ^ core) * half + part // sub * share + row % share
                x_ref[pl.ds(pl.multiple_of(place, piece), piece), :] = block[pl.ds(i * piece, piece), :]

        def columns(weight, out):
            for begin in range(0, hidden_cols, 512):
                width = min(512, hidden_cols - begin)
                product = jnp.dot(x_ref[...], weight[:, begin : begin + width], preferred_element_type=jnp.float32)
                cols = pl.ds(out + begin, width)
                keep_ref[:, cols] = product[:half]
                send_ref[:, cols] = product[half:].astype(send_ref.dtype)

        columns(gate_ref, 0)
        rest.wait()
        columns(up_ref, hidden_cols)

    shape = (half, 2 * hidden_cols)
    return pl.pallas_call(
        kernel,
        out_shape=[
            jax.ShapeDtypeStruct(shape, jnp.float32),
            jax.ShapeDtypeStruct(shape, jnp.bfloat16),
            pltpu.VMEM((depth, hidden_cols), jnp.bfloat16),
        ],
        in_specs=[VMEM] * (wide + 1) + [pl.BlockSpec(memory_space=pltpu.HBM), VMEM, VMEM],
        input_output_aliases={wide + 2: 2},
        out_specs=[VMEM] * 3,
        scratch_shapes=[pltpu.VMEM((rows, depth), jnp.bfloat16), pltpu.SemaphoreType.DMA(())],
        compiler_params=PARAMS,
        name="forward",
    )(*blocks, gate_weight, up_weight, up_buffer, held)


def activate(own, others, grads, sizes):
    wide, narrow, sub = sizes
    rows, both = own.shape
    hidden_cols = both // 2
    share = rows // narrow

    def kernel(*refs):
        own_ref = refs[0]
        other_refs = refs[1:narrow]
        grad_refs = refs[narrow : 2 * narrow]
        hidden_ref, pre_ref = refs[2 * narrow :]
        me = lax.axis_index("narrow")
        for step, grad_ref in enumerate(grad_refs):
            row = pl.ds(pl.multiple_of(source(me, step, narrow) * share, share), share)

            def total(cols, row=row):
                value = own_ref[row, cols]
                for other in other_refs:
                    value += other[row, cols].astype(jnp.float32)
                return value

            for start in range(0, hidden_cols, 128):
                cols = pl.ds(start, 128)
                up_cols = pl.ds(start + hidden_cols, 128)
                gate, up = total(cols), total(up_cols)
                sig = 1.0 / (1.0 + jnp.exp(-gate))
                act = gate * sig
                if step == 0:
                    hidden_ref[:, cols] = (act * up).astype(jnp.bfloat16)
                grad = grad_ref[:, cols].astype(jnp.float32)
                pre_ref[row, cols] = (grad * up * sig * (1.0 + gate * (1.0 - sig))).astype(jnp.bfloat16)
                pre_ref[row, up_cols] = (grad * act).astype(jnp.bfloat16)

    return pl.pallas_call(
        kernel,
        out_shape=[
            pltpu.VMEM((share, hidden_cols), jnp.bfloat16),
            jax.ShapeDtypeStruct((rows, both), jnp.bfloat16),
        ],
        in_specs=[VMEM] * (2 * narrow),
        out_specs=[VMEM] * 2,
        compiler_params=PARAMS,
        name="activate",
    )(own, *others, *grads)


def backward(own, other, gate_turned, up_turned, begin, depth, groups, sizes):
    wide, narrow, sub = sizes
    half, both = own.shape
    hidden_cols = both // 2
    rows = half * sub
    block_rows = rows // wide
    share = half // narrow
    piece = math.gcd(block_rows, share)
    tile = math.gcd(depth, 1024)

    def kernel(own_ref, other_ref, gate_ref, up_ref, *refs):
        out_refs, pre_ref = refs[:-1], refs[-1]
        me, core = lax.axis_index("wide"), lax.axis_index("sub")
        for flip, ref in enumerate((own_ref, other_ref)):
            for i in range(half // piece):
                row = (i * piece // share * sub + (core ^ flip)) * share + i * piece % share
                place = source(row // block_rows, me, wide) * block_rows + row % block_rows
                pre_ref[pl.ds(pl.multiple_of(place, piece), piece), :] = ref[pl.ds(i * piece, piece), :]

        for start in range(0, depth, tile):
            from_cols, cols = pl.ds(begin + start, tile), pl.ds(start, tile)
            product = jnp.dot(pre_ref[:, :hidden_cols], gate_ref[:, from_cols], preferred_element_type=jnp.float32)
            product += jnp.dot(pre_ref[:, hidden_cols:], up_ref[:, from_cols], preferred_element_type=jnp.float32)
            for (steps, dtype), out in zip(groups, out_refs):
                for i, step in enumerate(steps):
                    block = product[step * block_rows : (step + 1) * block_rows].astype(dtype)
                    out[i * block_rows : (i + 1) * block_rows, cols] = block

    return pl.pallas_call(
        kernel,
        out_shape=[jax.ShapeDtypeStruct((len(steps) * block_rows, depth), dtype) for steps, dtype in groups],
        in_specs=[VMEM] * 4,
        out_specs=[VMEM] * len(groups),
        scratch_shapes=[pltpu.VMEM((rows, both), jnp.bfloat16)],
        compiler_params=PARAMS,
        cost_estimate=pl.CostEstimate(
            flops=2 * rows * both * depth, bytes_accessed=2 * both * depth, transcendentals=0
        ),
        name="backward",
    )(own, other, gate_turned, up_turned)


def shards(tokens, gate_weight, up_weight, hidden_grad, sizes):
    wide, narrow, sub = sizes
    order = [3, 2, 1] if wide == 4 else list(range(1, wide))
    got = {step: exchange(tokens, "wide", step, wide) for step in order}
    steps = [0] + order
    blocks = [tokens] + [got[step] for step in order]
    gate_weight = pltpu.with_memory_space_constraint(gate_weight, pltpu.HBM)
    up_weight = pltpu.with_memory_space_constraint(up_weight, pltpu.HBM)
    grads = [hidden_grad] + [exchange(hidden_grad, "narrow", step, narrow) for step in range(1, narrow)]
    gate_weight, gate_turned, up_buffer = load_turned(gate_weight, up_weight)
    blocks, grads = lax.optimization_barrier((blocks, grads))
    keep, send, up_weight = forward(steps, blocks, gate_weight, up_weight, up_buffer, gate_turned, sizes)
    chip = keep + exchange(send, "sub", 1, sub).astype(jnp.float32)
    chip_bf16 = chip.astype(jnp.bfloat16)
    up_weight, chip_bf16 = lax.optimization_barrier((up_weight, chip_bf16))
    others = [exchange(chip_bf16, "narrow", step, narrow) for step in range(1, narrow)]
    up_turned = turn(up_weight)
    others, up_turned = lax.optimization_barrier((others, up_turned))
    hidden, pre = activate(chip, others, grads, sizes)
    pre_other = exchange(pre, "sub", 1, sub)

    order = list(range(1, wide))
    f32, bf16 = jnp.float32, jnp.bfloat16
    bwd = functools.partial(backward, pre, pre_other, gate_turned, up_turned, sizes=sizes)
    direct = [((0,), f32)] + [((step,), bf16) for step in order]
    width = tokens.shape[1] // PARTS
    totals = []
    for part in range(PARTS):
        own, *sends = bwd(begin=part * width, depth=width, groups=direct)
        sends = dict(zip(order, sends))
        turns = [3, 1, 2] if wide == 4 else order
        got = [exchange(sends[step], "wide", step, wide) for step in turns]
        totals.append(own + sum(x.astype(f32) for x in got))
    return (hidden, jnp.concatenate([total.astype(bf16) for total in totals], axis=1))


def solution(mesh):
    sizes = tuple(mesh.shape[axis] for axis in ("wide", "narrow", "sub"))
    return jax.shard_map(
        functools.partial(shards, sizes=sizes),
        mesh=mesh,
        in_specs=(
            P(("groups", "wide"), ("narrow", "sub")),
            P(("narrow", "sub"), "wide"),
            P(("narrow", "sub"), "wide"),
            P(("groups", "narrow", "sub"), "wide"),
        ),
        out_specs=(
            P(("groups", "narrow", "sub"), "wide"),
            P(("groups", "wide"), ("narrow", "sub")),
        ),
        check_vma=False,
    )
```

```python
import functools
import math

import jax
import jax.numpy as jnp
from jax import lax
from jax.experimental import pallas as pl
from jax.experimental.pallas import tpu as pltpu
from jax.sharding import PartitionSpec as P

VMEM = pl.BlockSpec(memory_space=pltpu.VMEM)
PARAMS = pltpu.CompilerParams(vmem_limit_bytes=8 << 20)
PARTS = 2


def partner(index, step, size):
    return index ^ step if size & (size - 1) == 0 else (index + step) % size


def source(index, step, size):
    return index ^ step if size & (size - 1) == 0 else (index + size - step) % size


def exchange(x, axis, step, size):
    return lax.ppermute(x, axis, [(i, partner(i, step, size)) for i in range(size)])


def load_turned(weight, next_weight, step=512):
    depth, hidden_cols = weight.shape
    step = math.gcd(depth, step)
    parts = depth // step
    ahead = ahead_rows(depth)

    def kernel(hbm_ref, next_hbm, out_ref, turned_ref, next_ref, sems):
        def copy(part):
            span = pl.ds(pl.multiple_of(part * step, step), step)
            return pltpu.make_async_copy(hbm_ref.at[span], out_ref.at[span], sems.at[part])

        for part in range(parts):
            copy(part).start()
        next_copy = pltpu.make_async_copy(next_hbm.at[pl.ds(0, ahead)], next_ref.at[pl.ds(0, ahead)], sems.at[parts])
        next_copy.start()

        def body(part, carry):
            span = pl.ds(pl.multiple_of(part * step, step), step)
            copy(part).wait()
            turned_ref[:, span] = out_ref[span, :].T
            return carry

        lax.fori_loop(0, parts, body, 0)
        next_copy.wait()

    shape = pltpu.VMEM((depth, hidden_cols), jnp.bfloat16)
    return pl.pallas_call(
        kernel,
        out_shape=[shape, pltpu.VMEM((hidden_cols, depth), jnp.bfloat16), shape],
        in_specs=[pl.BlockSpec(memory_space=pltpu.HBM)] * 2,
        out_specs=[VMEM] * 3,
        scratch_shapes=[pltpu.SemaphoreType.DMA((parts + 1,))],
        compiler_params=PARAMS,
        cost_estimate=pl.CostEstimate(flops=0, bytes_accessed=2 * weight.size, transcendentals=0),
        name="load_turned",
    )(weight, next_weight)


def ahead_rows(depth):
    return depth * 5 // 8


def turn(weight, step=2048):
    depth, hidden_cols = weight.shape
    step = math.gcd(depth, step)

    def kernel(weight_ref, out_ref):
        def body(part, carry):
            span = pl.ds(pl.multiple_of(part * step, step), step)
            out_ref[:, span] = weight_ref[span, :].T
            return carry

        lax.fori_loop(0, depth // step, body, 0)

    return pl.pallas_call(
        kernel,
        out_shape=pltpu.VMEM((hidden_cols, depth), jnp.bfloat16),
        in_specs=[VMEM],
        out_specs=VMEM,
        compiler_params=PARAMS,
        cost_estimate=pl.CostEstimate(flops=0, bytes_accessed=2 * 2 * weight.size, transcendentals=0),
        name="turn",
    )(weight)


def forward(steps, blocks, gate_weight, up_weight, up_buffer, held, sizes):
    wide, narrow, sub = sizes
    block_rows, depth = blocks[0].shape
    hidden_cols = gate_weight.shape[1]
    rows = block_rows * wide
    share = rows // (narrow * sub)
    piece = math.gcd(block_rows, share)
    half = rows // sub
    ahead = ahead_rows(depth)

    def kernel(*refs):
        block_refs = refs[:wide]
        gate_ref, up_hbm, _, _, keep_ref, send_ref, up_ref, x_ref, sem = refs[wide:]
        span = pl.ds(ahead, depth - ahead)
        rest = pltpu.make_async_copy(up_hbm.at[span], up_ref.at[span], sem)
        rest.start()
        me, core = lax.axis_index("wide"), lax.axis_index("sub")
        for step, block in zip(steps, block_refs):
            owner = source(me, step, wide)
            for i in range(block_rows // piece):
                row = owner * block_rows + i * piece
                part = row // share
                place = ((part % sub) ^ core) * half + part // sub * share + row % share
                x_ref[pl.ds(pl.multiple_of(place, piece), piece), :] = block[pl.ds(i * piece, piece), :]

        def columns(weight, out):
            for begin in range(0, hidden_cols, 512):
                width = min(512, hidden_cols - begin)
                product = jnp.dot(x_ref[...], weight[:, begin : begin + width], preferred_element_type=jnp.float32)
                cols = pl.ds(out + begin, width)
                keep_ref[:, cols] = product[:half]
                send_ref[:, cols] = product[half:].astype(send_ref.dtype)

        columns(gate_ref, 0)
        rest.wait()
        columns(up_ref, hidden_cols)

    shape = (half, 2 * hidden_cols)
    return pl.pallas_call(
        kernel,
        out_shape=[
            jax.ShapeDtypeStruct(shape, jnp.float32),
            jax.ShapeDtypeStruct(shape, jnp.bfloat16),
            pltpu.VMEM((depth, hidden_cols), jnp.bfloat16),
        ],
        in_specs=[VMEM] * (wide + 1) + [pl.BlockSpec(memory_space=pltpu.HBM), VMEM, VMEM],
        input_output_aliases={wide + 2: 2},
        out_specs=[VMEM] * 3,
        scratch_shapes=[pltpu.VMEM((rows, depth), jnp.bfloat16), pltpu.SemaphoreType.DMA(())],
        compiler_params=PARAMS,
        name="forward",
    )(*blocks, gate_weight, up_weight, up_buffer, held)


def activate(own, others, grads, sizes):
    wide, narrow, sub = sizes
    rows, both = own.shape
    hidden_cols = both // 2
    share = rows // narrow

    def kernel(*refs):
        own_ref = refs[0]
        other_refs = refs[1:narrow]
        grad_refs = refs[narrow : 2 * narrow]
        hidden_ref, pre_ref = refs[2 * narrow :]
        me = lax.axis_index("narrow")
        for step, grad_ref in enumerate(grad_refs):
            row = pl.ds(pl.multiple_of(source(me, step, narrow) * share, share), share)

            def total(cols, row=row):
                value = own_ref[row, cols]
                for other in other_refs:
                    value += other[row, cols].astype(jnp.float32)
                return value

            for start in range(0, hidden_cols, 128):
                cols = pl.ds(start, 128)
                up_cols = pl.ds(start + hidden_cols, 128)
                gate, up = total(cols), total(up_cols)
                sig = 1.0 / (1.0 + jnp.exp(-gate))
                act = gate * sig
                if step == 0:
                    hidden_ref[:, cols] = (act * up).astype(jnp.bfloat16)
                grad = grad_ref[:, cols].astype(jnp.float32)
                pre_ref[row, cols] = (grad * up * sig * (1.0 + gate * (1.0 - sig))).astype(jnp.bfloat16)
                pre_ref[row, up_cols] = (grad * act).astype(jnp.bfloat16)

    return pl.pallas_call(
        kernel,
        out_shape=[
            pltpu.VMEM((share, hidden_cols), jnp.bfloat16),
            jax.ShapeDtypeStruct((rows, both), jnp.bfloat16),
        ],
        in_specs=[VMEM] * (2 * narrow),
        out_specs=[VMEM] * 2,
        compiler_params=PARAMS,
        name="activate",
    )(own, *others, *grads)


def backward(own, other, gate_turned, up_turned, begin, depth, groups, sizes):
    wide, narrow, sub = sizes
    half, both = own.shape
    hidden_cols = both // 2
    rows = half * sub
    block_rows = rows // wide
    share = half // narrow
    piece = math.gcd(block_rows, share)
    tile = math.gcd(depth, 1024)

    def kernel(own_ref, other_ref, gate_ref, up_ref, *refs):
        out_refs, pre_ref = refs[:-1], refs[-1]
        me, core = lax.axis_index("wide"), lax.axis_index("sub")
        for flip, ref in enumerate((own_ref, other_ref)):
            for i in range(half // piece):
                row = (i * piece // share * sub + (core ^ flip)) * share + i * piece % share
                place = source(row // block_rows, me, wide) * block_rows + row % block_rows
                pre_ref[pl.ds(pl.multiple_of(place, piece), piece), :] = ref[pl.ds(i * piece, piece), :]

        for start in range(0, depth, tile):
            from_cols, cols = pl.ds(begin + start, tile), pl.ds(start, tile)
            product = jnp.dot(pre_ref[:, :hidden_cols], gate_ref[:, from_cols], preferred_element_type=jnp.float32)
            product += jnp.dot(pre_ref[:, hidden_cols:], up_ref[:, from_cols], preferred_element_type=jnp.float32)
            for (steps, dtype), out in zip(groups, out_refs):
                for i, step in enumerate(steps):
                    block = product[step * block_rows : (step + 1) * block_rows].astype(dtype)
                    out[i * block_rows : (i + 1) * block_rows, cols] = block

    return pl.pallas_call(
        kernel,
        out_shape=[jax.ShapeDtypeStruct((len(steps) * block_rows, depth), dtype) for steps, dtype in groups],
        in_specs=[VMEM] * 4,
        out_specs=[VMEM] * len(groups),
        scratch_shapes=[pltpu.VMEM((rows, both), jnp.bfloat16)],
        compiler_params=PARAMS,
        cost_estimate=pl.CostEstimate(
            flops=2 * rows * both * depth, bytes_accessed=2 * both * depth, transcendentals=0
        ),
        name="backward",
    )(own, other, gate_turned, up_turned)


def shards(tokens, gate_weight, up_weight, hidden_grad, sizes):
    wide, narrow, sub = sizes
    order = [2, 3, 1] if wide == 4 else list(range(1, wide))
    got = {step: exchange(tokens, "wide", step, wide) for step in order}
    steps = [0] + order
    blocks = [tokens] + [got[step] for step in order]
    gate_weight = pltpu.with_memory_space_constraint(gate_weight, pltpu.HBM)
    up_weight = pltpu.with_memory_space_constraint(up_weight, pltpu.HBM)
    grads = [hidden_grad] + [exchange(hidden_grad, "narrow", step, narrow) for step in range(1, narrow)]
    gate_weight, gate_turned, up_buffer = load_turned(gate_weight, up_weight)
    blocks, grads = lax.optimization_barrier((blocks, grads))
    keep, send, up_weight = forward(steps, blocks, gate_weight, up_weight, up_buffer, gate_turned, sizes)
    chip = keep + exchange(send, "sub", 1, sub).astype(jnp.float32)
    chip_bf16 = chip.astype(jnp.bfloat16)
    up_weight, chip_bf16 = lax.optimization_barrier((up_weight, chip_bf16))
    others = [exchange(chip_bf16, "narrow", step, narrow) for step in range(1, narrow)]
    up_turned = turn(up_weight)
    others, up_turned = lax.optimization_barrier((others, up_turned))
    hidden, pre = activate(chip, others, grads, sizes)
    pre_other = exchange(pre, "sub", 1, sub)

    order = list(range(1, wide))
    f32, bf16 = jnp.float32, jnp.bfloat16
    bwd = functools.partial(backward, pre, pre_other, gate_turned, up_turned, sizes=sizes)
    direct = [((0,), f32)] + [((step,), bf16) for step in order]
    width = tokens.shape[1] // PARTS
    totals = []
    for part in range(PARTS):
        own, *sends = bwd(begin=part * width, depth=width, groups=direct)
        sends = dict(zip(order, sends))
        turns = ([3, 1, 2], [2, 3, 1])[part] if wide == 4 else order
        got = [exchange(sends[step], "wide", step, wide) for step in turns]
        totals.append(own + sum(x.astype(f32) for x in got))
    return (hidden, jnp.concatenate([total.astype(bf16) for total in totals], axis=1))


def solution(mesh):
    sizes = tuple(mesh.shape[axis] for axis in ("wide", "narrow", "sub"))
    return jax.shard_map(
        functools.partial(shards, sizes=sizes),
        mesh=mesh,
        in_specs=(
            P(("groups", "wide"), ("narrow", "sub")),
            P(("narrow", "sub"), "wide"),
            P(("narrow", "sub"), "wide"),
            P(("groups", "narrow", "sub"), "wide"),
        ),
        out_specs=(
            P(("groups", "narrow", "sub"), "wide"),
            P(("groups", "wide"), ("narrow", "sub")),
        ),
        check_vma=False,
    )
```
